512 devices in a mesh: row: 32 (over z, x), col: 16 (over y, core).
Axes of the slice: x: 4, y: 8, z: 8, core: 2. Of those that a mesh axis runs over, the one named last changes fastest.
Arguments:
- covariance: float32 [16384, 16384], P('row', 'col'), as said below
Outputs:
- factored: float32 [16384, 16384], P('row', 'col')
Inputs may be any that keep to these rules, and one draw needn't show every extreme that they name: covariance is symmetric and positive definite in natural order, with smallest eigenvalue well above zero.
All inputs are finite; a program needn't handle non-finite values.
Results may differ from the reference program's by a relative error of at most 0.0001.
Values sent between devices are 32-bit elements; how exact they have to be, the bound alone decides.
No kernel may reach another device: no remote copies, remote signals or barrier semaphores. Data moves between devices by JAX's collectives and lax.ppermute only.
A program may use at most 64 MiB of HBM per device.

```python
import jax
import jax.numpy as jnp
from jax import lax

W = 16384
NB = 256
STEPS = 2
ROW_BLOCKS = 2
COL_BLOCKS = 4
N_ROW = 32
N_COL = 16


def draw_covariance(key, part):
    key = jax.random.fold_in(key, 11)
    key_factor, key_scale, key_noise, key_diag = jax.random.split(key, 4)
    inner = STEPS * NB
    scales = jnp.exp(jax.random.uniform(key_scale, (W,), jnp.float32, jnp.log(0.5), jnp.log(2.0)))
    loading = jax.random.normal(key_factor, (W, inner), jnp.float32) * scales[:, None] / jnp.sqrt(jnp.float32(inner))
    shared = jnp.dot(loading, loading.T, precision=lax.Precision.HIGHEST, preferred_element_type=jnp.float32)
    noise = jax.random.uniform(key_noise, (W, W), jnp.float32, -1.0, 1.0)
    noise = (noise + noise.T) * (0.3 / jnp.sqrt(jnp.float32(W)))
    diagonal = jax.random.uniform(key_diag, (W,), jnp.float32, 1.5, 2.5)
    matrix = shared + noise + jnp.diag(diagonal)
    shaped = matrix.reshape(ROW_BLOCKS, N_ROW, NB, COL_BLOCKS, N_COL, NB)
    return shaped.transpose(1, 0, 2, 4, 3, 5).reshape(W, W).astype(jnp.float32)


def setup_inputs(seed: int = 0) -> dict:
    streams_of = jax.random.split(jax.random.key(seed), 2)
    return {
        "covariance": draw_covariance(jax.random.fold_in(streams_of[1], 71), 0),
    }


def to_natural(stored):
    shaped = stored.reshape(N_ROW, ROW_BLOCKS, NB, N_COL, COL_BLOCKS, NB)
    return shaped.transpose(1, 0, 2, 4, 3, 5).reshape(W, W)

def to_storage(matrix):
    shaped = matrix.reshape(ROW_BLOCKS, N_ROW, NB, COL_BLOCKS, N_COL, NB)
    return shaped.transpose(1, 0, 2, 4, 3, 5).reshape(W, W)

def reference(covariance):
    matrix = to_natural(covariance)
    for step in range(STEPS):
        first_col = step * NB
        corner = matrix[first_col:first_col + NB, first_col:first_col + NB]
        factor = jnp.linalg.cholesky(corner)
        below = matrix[first_col + NB:, first_col:first_col + NB]
        solved = jax.scipy.linalg.solve_triangular(factor, below.T, lower=True).T
        update = jnp.dot(solved.astype(jnp.float32), solved.T.astype(jnp.float32), precision=lax.Precision.HIGHEST, preferred_element_type=jnp.float32)
        matrix = matrix.at[first_col + NB:, first_col + NB:].add(-update)
        matrix = matrix.at[first_col:first_col + NB, first_col:first_col + NB].set(factor)
        matrix = matrix.at[first_col + NB:, first_col:first_col + NB].set(solved)
        matrix = matrix.at[first_col:first_col + NB, first_col + NB:].set(0.0)
    return to_storage(matrix)
```

```python
import functools

import jax
import jax.numpy as jnp
import numpy as np
from jax import lax
from jax.experimental import pallas as pl
from jax.experimental.pallas import tpu as pltpu
from jax.sharding import PartitionSpec as P

NB = 256
PANEL = 512
NZ, NX, NY, NK = 8, 4, 8, 2
B = 128
S = 8
F32 = jnp.float32
BOTH = ("row", "col")


def dot(a, b, dims):
    return lax.dot_general(a, b, (dims, ((), ())), precision=lax.Precision.HIGHEST, preferred_element_type=F32)


def device(z, x, y, k):
    return (((z % NZ) * NX + x % NX) * NY + y % NY) * NK + k


DEVICES = [(z, x, y, k) for z in range(NZ) for x in range(NX) for y in range(NY) for k in range(NK)]


def send(value, target):
    pairs = []
    for at in DEVICES:
        to = target(*at)
        if to is not None:
            pairs.append((device(*at), device(*to)))
    return lax.ppermute(value, BOTH, pairs)


HOPS = [({0: 3}, {0: 5}), ({0: 1, 3: 4, 5: 6}, {0: 7, 3: 2})]


def along_y(part, where=lambda z, x, k: True):
    return lambda z, x, y, k: (z, x, part[y], k) if y in part and where(z, x, k) else None


def along_z(part, where=lambda x, y, k: True):
    return lambda z, x, y, k: (part[z], x, y, k) if z in part and where(x, y, k) else None


def pair_x(where):
    other = {0: 3, 1: 2}
    return lambda z, x, y, k: (z, other[x], y, k) if x in other and where(z, y, k) else None


def either(first, second):
    def target(z, x, y, k):
        return (second if k else first)(z, x, y, k)

    return target


def nowhere(z, x, y, k):
    return None


def spread_corner(block, row, col):
    core = col
    blocks = [block[:B, :B], block[B:, :B], block[B:, B:]]
    diagonal = row == core
    half = [jnp.where(core == 0, blocks[0], blocks[1]), jnp.where(core == 0, blocks[1], blocks[2]), blocks[2]]
    mine = jnp.concatenate([jnp.where(diagonal, t, h) for t, h in zip(blocks, half)])
    theirs = send(mine, lambda z, x, y, k: (z, 1 - x, y, k) if z == 0 and x < 2 and y == 0 else None)
    piece = jnp.concatenate([jnp.where(diagonal, mine, theirs), jnp.where(diagonal, theirs, mine)[: 2 * B]])
    piece = jnp.where((row < 2) & (col < 2), piece, 0.0)
    left = lambda z, x, k: z == 0 and x < 2
    rounds = [
        [(along_y(HOPS[0][s], left), along_z(HOPS[0][s], lambda x, y, k: x < 2 and y == 0)) for s in (0, 1)],
        [(along_y(HOPS[1][s], left), along_z(HOPS[1][s], lambda x, y, k: x < 2 and y == 0)) for s in (0, 1)],
        [
            (along_z(HOPS[0][0], lambda x, y, k: x < 2), pair_x(lambda z, y, k: y == 0)),
            (along_z(HOPS[0][1], lambda x, y, k: x < 2), nowhere),
        ],
        [(along_z(HOPS[1][s], lambda x, y, k: x < 2), along_y(HOPS[0][s])) for s in (0, 1)],
        [
            (pair_x(lambda z, y, k: True), along_y(HOPS[1][0])),
            (nowhere, along_y(HOPS[1][1])),
        ],
    ]
    for steps in rounds:
        got = [send(piece, either(*step)) for step in steps]
        piece = piece + got[0] + got[1]
    other = send(piece, lambda z, x, y, k: (z, x, y, 1 - k))
    return piece, other


def spread_rows(top):
    half = top.shape[1] // 2
    x_index = lax.axis_index("row") % NX
    far = send(top[:, half:], pair_x(lambda z, y, k: z == 0))
    quarter = jnp.where(x_index < 2, top[:, :half], far)
    quarter = jnp.where(lax.axis_index("row") < NX, quarter, 0.0)
    for hops in HOPS:
        got = [send(quarter, along_z(hop)) for hop in hops]
        quarter = quarter + got[0] + got[1]
    behind = send(quarter, lambda z, x, y, k: (z, x + 1, y, k))
    ahead = send(quarter, lambda z, x, y, k: (z, x - 1, y, k))
    low = send(behind[: NB // 2], lambda z, x, y, k: (z, x + 1, y, k))
    high = send(ahead[NB // 2 :], lambda z, x, y, k: (z, x - 1, y, k))
    return quarter, behind, ahead, low, high


def spread_cols(left):
    left = jnp.where(lax.axis_index("col") < NK, left, 0.0)
    for hops in HOPS:
        got = [send(left, along_y(hop)) for hop in hops]
        left = left + got[0] + got[1]
    other = send(left, lambda z, x, y, k: (z, x, y, 1 - k))
    return left, other


def factor_block(d, up, inv):
    lane = lax.broadcasted_iota(jnp.int32, (S, B), 1)
    sub = lax.broadcasted_iota(jnp.int32, (S, B), 0)

    def stack(rows):
        out = rows[0]
        for i in range(1, S):
            out = jnp.where(sub == i, rows[i], out)
        return out

    for k in range(0, B, S):
        here = (lane >= k) & (lane < k + S)
        p = [jnp.broadcast_to(d[k + i : k + i + 1, :], (S, B)) for i in range(S)]
        s = {(i, j): jnp.broadcast_to(p[i][:, k + j : k + j + 1], (S, B)) for i in range(S) for j in range(i + 1)}
        r, w = [], {}
        for j in range(S):
            r.append(lax.rsqrt(s[j, j]))
            for i in range(j + 1, S):
                s[i, j] = s[i, j] * r[j]
            for i in range(j + 1, S):
                for m in range(j + 1, i + 1):
                    s[i, m] = s[i, m] - s[i, j] * s[m, j]
            w[j, j] = r[j]
            for m in range(j):
                acc = s[j, m] * w[m, m]
                for q in range(m + 1, j):
                    acc = acc + s[j, q] * w[q, m]
                w[j, m] = -r[j] * acc
        q = [jnp.where(here, jnp.where(lane == k + i, 1.0, 0.0), p[i]) for i in range(S)]
        u, t = [], []
        for i in range(S):
            a = w[i, 0] * q[0]
            b = w[i, 0] * p[0]
            for m in range(1, i + 1):
                a = a + w[i, m] * q[m]
                b = b + w[i, m] * p[m]
            u.append(a)
            t.append(b)
        up[k : k + S, :] = jnp.where(lane >= k + sub, stack(t), 0.0)
        inv[k : k + S, :] = jnp.where(lane <= k + sub, stack(u), 0.0)
        rest = B - k - S
        if rest:
            below = d[k + S :, :]
            groups = rest // S
            new = jnp.where(here[None], 0.0, below.reshape(groups, S, B))
            for i in range(S):
                v = w[i, i] * u[i]
                for m in range(i + 1, S):
                    v = v + w[m, i] * u[m]
                c = jnp.broadcast_to(below[:, k + i : k + i + 1], (rest, B)).reshape(groups, S, B)
                new = new - c * v[None]
            d[k + S :, :] = new.reshape(rest, B)


def factor_kernel(place, own, other, low_ref, inv_ref, a, d, up, wi):
    n = PANEL
    first = place[3] == 0
    block = lambda ref, i: ref[i * B : (i + 1) * B, :]
    p0 = [jnp.where(first, block(own, i), block(other, i)) for i in range(5)]
    p1 = [jnp.where(first, block(other, i), block(own, i)) for i in range(5)]
    lower = {
        (0, 0): p0[0], (1, 0): p0[1], (1, 1): p0[2],
        (2, 2): p1[0], (3, 2): p1[1], (3, 3): p1[2],
        (2, 0): p0[3], (3, 0): p0[4], (2, 1): p1[3].T, (3, 1): p1[4].T,
    }
    for (i, j), value in lower.items():
        a[i * B : (i + 1) * B, j * B : (j + 1) * B] = value
        if i != j:
            a[j * B : (j + 1) * B, i * B : (i + 1) * B] = value.T
    low_ref[...] = jnp.zeros_like(low_ref)
    inv_ref[...] = jnp.zeros_like(inv_ref)
    row = lax.broadcasted_iota(jnp.int32, (n, B), 0)

    def step(ob, _):
        at = pl.multiple_of(ob * B, B)
        blk = pl.ds(at, B)
        d[...] = a[blk, blk]
        factor_block(d, up, wi)
        w = wi[...]
        inv_ref[blk, blk] = w
        x = jnp.where(row >= at + B, dot(a[:, blk], w, ((1,), (1,))), 0.0)
        low_ref[:, blk] = x
        low_ref[blk, blk] = up[...].T
        a[...] = a[...] - dot(x, x, ((1,), (1,)))
        return 0

    lax.fori_loop(0, n // B, step, 0)
    size = B
    while size < n:
        for at in range(0, n, 2 * size):
            lo, hi = pl.ds(at, size), pl.ds(at + size, size)
            mid = dot(low_ref[hi, lo], inv_ref[lo, lo], ((1,), (0,)))
            inv_ref[hi, lo] = -dot(inv_ref[hi, hi], mid, ((1,), (0,)))
        size *= 2


def left_kernel(place, inv, own, other, x_ref, k_ref):
    first = place[3] == 0
    p0 = jnp.where(first, own[...], other[...])
    p1 = jnp.where(first, other[...], own[...])
    x_ref[...] = dot(p0, inv[:, :NB], ((1,), (1,))) + dot(p1, inv[:, NB:], ((1,), (1,)))
    k_ref[...] = dot(x_ref[...], inv[...], ((1,), (0,)))


def update_kernel(place, a, left, solved, low, here, behind, ahead, far0, far1, out):
    row, col, x = place[0], place[1], place[2]
    half = here.shape[1]
    out[...] = a[...]

    def apply(q, values, part, count):
        at = pl.multiple_of(jnp.where(q < 2, 0, half), half)
        depth = pl.multiple_of(jnp.where((q == 0) | (q == 3), 0, NB) + part, B)
        out[:, pl.ds(at, half)] -= dot(left[:, pl.ds(depth, count)], values[...], ((1,), (0,)))

    apply(x, here, 0, NB)
    apply(lax.rem(x + 3, 4), behind, 0, NB)
    apply(lax.rem(x + 1, 4), ahead, 0, NB)
    apply(lax.rem(x + 2, 4), far0, 0, NB // 2)
    apply(lax.rem(x + 2, 4), far1, NB // 2, NB // 2)

    @pl.when(col < 2)
    def _():
        out[:, :NB] = solved[:, pl.ds(pl.multiple_of(col * NB, NB), NB)]

    @pl.when(row < 2)
    def _():
        out[:NB, :] = jnp.zeros((NB, out.shape[1]), F32)

    @pl.when((row < 2) & (col < 2))
    def _():
        out[:NB, :NB] = low[pl.ds(pl.multiple_of(row * NB, NB), NB), pl.ds(pl.multiple_of(col * NB, NB), NB)]


def call(kernel, shapes, scratch, flops, *args):
    smem = pl.BlockSpec(memory_space=pltpu.SMEM)
    vmem = pl.BlockSpec(memory_space=pltpu.VMEM)
    moved = sum(int(np.prod(s)) for s in shapes) * 4 + sum(a.size for a in args) * 4
    outs = tuple(jax.ShapeDtypeStruct(s, F32) for s in shapes)
    return pl.pallas_call(
        kernel,
        out_shape=outs,
        in_specs=[smem] + [vmem] * (len(args) - 1),
        out_specs=tuple(vmem for _ in shapes),
        scratch_shapes=[pltpu.VMEM(s, F32) for s in scratch],
        compiler_params=pltpu.CompilerParams(vmem_limit_bytes=40 << 20),
        cost_estimate=pl.CostEstimate(flops=flops, bytes_accessed=moved, transcendentals=0),
    )(*args)


def on_device(matrix):
    row, col = lax.axis_index("row"), lax.axis_index("col")
    place = jnp.stack([row, col, row % NX, col % NK]).astype(jnp.int32)
    n, m = matrix.shape
    with jax.named_scope("corner"):
        corner = spread_corner(matrix[:NB, :NB], row, col)
    with jax.named_scope("rows"):
        rows = spread_rows(matrix[:NB, :])
    with jax.named_scope("cols"):
        cols = spread_cols(matrix[:, :NB])
    full = (PANEL, PANEL)
    low, inv = call(factor_kernel, [full, full], [full, (B, B), (B, B), (B, B)], 30_000_000_000, place, *corner)
    solved, left = call(left_kernel, [(n, PANEL), (n, PANEL)], [], 4 * n * PANEL * PANEL * 6, place, inv, *cols)
    (out,) = call(update_kernel, [(n, m)], [], 2 * n * m * PANEL * 6, place, matrix, left, solved, low, *rows)
    return out


def solution(mesh):
    return jax.shard_map(on_device, mesh=mesh, in_specs=(P("row", "col"),), out_specs=P("row", "col"), check_vma=False)
```

```python
import functools

import jax
import jax.numpy as jnp
import numpy as np
from jax import lax
from jax.experimental import pallas as pl
from jax.experimental.pallas import tpu as pltpu
from jax.sharding import PartitionSpec as P

NB = 256
PANEL = 512
NZ, NX, NY, NK = 8, 4, 8, 2
B = 128
S = 8
F32 = jnp.float32
BOTH = ("row", "col")


def dot(a, b, dims):
    return lax.dot_general(a, b, (dims, ((), ())), precision=lax.Precision.HIGHEST, preferred_element_type=F32)


def device(z, x, y, k):
    return (((z % NZ) * NX + x % NX) * NY + y % NY) * NK + k


DEVICES = [(z, x, y, k) for z in range(NZ) for x in range(NX) for y in range(NY) for k in range(NK)]


def send(value, target):
    pairs = []
    for at in DEVICES:
        to = target(*at)
        if to is not None:
            pairs.append((device(*at), device(*to)))
    return lax.ppermute(value, BOTH, pairs)


HOPS = [({0: 3}, {0: 5}), ({0: 1, 3: 4, 5: 6}, {0: 7, 3: 2})]


def along_y(part, where=lambda z, x, k: True):
    return lambda z, x, y, k: (z, x, part[y], k) if y in part and where(z, x, k) else None


def along_z(part, where=lambda x, y, k: True):
    return lambda z, x, y, k: (part[z], x, y, k) if z in part and where(x, y, k) else None


def along_x(part, where=lambda z, y, k: True):
    return lambda z, x, y, k: (z, part[x], y, k) if x in part and where(z, y, k) else None


def other_core(z, x, y, k):
    return z, x, y, 1 - k


def spread(value, targets, earlier=None):
    got = [send(value, target) for target in targets]
    if earlier is not None:
        got[0] = after(got[0], earlier)
    return functools.reduce(jnp.add, got, value)


def after(value, *earlier):
    return lax.optimization_barrier((value, *earlier))[0]


def corner_piece(block, row, col):
    blocks = [block[:B, :B], block[B:, :B], block[B:, B:]]
    first, second = [jnp.where(col == 0, x, y) for x, y in zip(blocks, blocks[1:])]
    mine = [jnp.where(row == col, t, h) for t, h in zip(blocks, (first, second, second))]
    return jnp.where((row < 2) & (col < 2), jnp.concatenate(mine), 0.0)


def pin(values, *earlier):
    return lax.optimization_barrier((tuple(values), earlier))[0]


def corner_tree(piece, quarter, sent, x_index, core):
    rounds = [
        [along_z(h, lambda x, y, k: x < 2 and y == 0) for h in HOPS[0]],
        [along_z(h, lambda x, y, k: x < 2 and y == 0) for h in HOPS[1]],
        [along_y(h, lambda z, x, k: x < 2) for h in HOPS[0]],
        [along_y(h, lambda z, x, k: x < 2) for h in HOPS[1]],
    ]
    piece = spread(piece, rounds[0])
    piece = spread(piece, rounds[1], sent)
    quarter = quarter(sent)
    piece = spread(piece, rounds[2])
    quarter = spread(quarter, [along_z(h) for h in HOPS[0]])
    piece = spread(piece, rounds[3], quarter)
    quarter = spread(quarter, [along_z(h) for h in HOPS[1]])
    swap, near, far = [send(piece, along_x(part)) for part in ({0: 1, 1: 0}, {0: 3, 1: 2}, {0: 2, 1: 3})]
    pick = lambda *choices: functools.reduce(lambda v, i: jnp.where(x_index == i, choices[i], v), (1, 2, 3), choices[0])
    even, odd = pick(piece, swap, far, near), pick(swap, piece, near, far)
    triangle = jnp.where(core == 0, even, odd)
    rest = jnp.where(core == 0, odd, even)[: 2 * B]
    mine = jnp.concatenate([triangle, rest])
    return piece, (mine, send(mine, other_core)), quarter


def factor_block(d, up, inv, tasks=()):
    lane = lax.broadcasted_iota(jnp.int32, (S, B), 1)
    sub = lax.broadcasted_iota(jnp.int32, (S, B), 0)
    panels = B // S
    tasks = list(tasks)

    def stack(rows):
        out = rows[0]
        for i in range(1, S):
            out = jnp.where(sub == i, rows[i], out)
        return out

    for done, k in enumerate(range(0, B, S)):
        here = (lane >= k) & (lane < k + S)
        p = [jnp.broadcast_to(d[k + i : k + i + 1, :], (S, B)) for i in range(S)]
        spare = B + done % 2 * S * S
        for j in range(S):
            d[spare + j * S : spare + (j + 1) * S, :] = jnp.broadcast_to(d[k : k + S, k + j : k + j + 1], (S, B))
        element = lambda i, j: d[spare + j * S + i : spare + j * S + i + 1, :]
        s = {(i, j): jnp.broadcast_to(element(i, j), (S, B)) for i in range(S) for j in range(i + 1)}
        r, w = [], {}
        for j in range(S):
            r.append(lax.rsqrt(s[j, j]))
            for i in range(j + 1, S):
                s[i, j] = s[i, j] * r[j]
            for i in range(j + 1, S):
                for m in range(j + 1, i + 1):
                    s[i, m] = s[i, m] - s[i, j] * s[m, j]
            w[j, j] = r[j]
            for m in range(j):
                acc = s[j, m] * w[m, m]
                for q in range(m + 1, j):
                    acc = acc + s[j, q] * w[q, m]
                w[j, m] = -r[j] * acc
        q = [jnp.where(here, jnp.where(lane == k + i, 1.0, 0.0), p[i]) for i in range(S)]
        u, t = [], []
        for i in range(S):
            a = w[i, 0] * q[0]
            b = w[i, 0] * p[0]
            for m in range(1, i + 1):
                a = a + w[i, m] * q[m]
                b = b + w[i, m] * p[m]
            u.append(a)
            t.append(b)
        up[k : k + S, :] = jnp.where(lane >= k + sub, stack(t), 0.0)
        inv[k : k + S, :] = jnp.where(lane <= k + sub, stack(u), 0.0)
        rest = B - k - S
        if rest:
            below = d[k + S : B, :]
            groups = rest // S
            new = jnp.where(here[None], 0.0, below.reshape(groups, S, B))
            for i in range(S):
                v = w[i, i] * u[i]
                for m in range(i + 1, S):
                    v = v + w[m, i] * u[m]
                c = jnp.broadcast_to(below[:, k + i : k + i + 1], (rest, B)).reshape(groups, S, B)
                new = new - c * v[None]
            d[k + S : B, :] = new.reshape(rest, B)
        for task in tasks[len(tasks) * done // panels : len(tasks) * (done + 1) // panels]:
            task()


def at(i, j):
    return pl.ds(i * B, B), pl.ds(j * B, B)


def outer(a, b):
    return dot(a, b, ((1,), (1,)))


def inner(a, b):
    return dot(a, b, ((1,), (0,)))


def below_task(a, low, inv, i, j):
    def task():
        low[at(i, j)] = outer(a[at(i, j)], inv[at(j, j)])

    return task


def trail_task(a, low, i, j, p):
    def task():
        a[at(i, j)] = a[at(i, j)] - outer(low[at(i, p)], low[at(j, p)])

    return task


def upto(i):
    return pl.ds(0, i * B)


def gather_task(low, inv, mid, i):
    def task():
        mid[:, upto(i)] = inner(low[pl.ds(i * B, B), upto(i)], inv[upto(i), upto(i)])

    return task


def invert_task(inv, mid, i):
    def task():
        inv[pl.ds(i * B, B), upto(i)] = -inner(inv[at(i, i)], mid[:, upto(i)])

    return task


def factor_step(i, low, inv, a, d, up, tasks):
    d[:B, :] = a[at(i, i)]
    factor_block(d, up, inv.at[at(i, i)], tasks)
    low[at(i, i)] = up[...].T
    if i < 3:
        below_task(a, low, inv, i + 1, i)()
        trail_task(a, low, i + 1, i + 1, i)()


def first_kernel(place, own, other, low, inv, a, d, up):
    first = place[3] == 0
    block = lambda ref, i: ref[i * B : (i + 1) * B, :]
    p0 = [jnp.where(first, block(own, i), block(other, i)) for i in range(5)]
    p1 = [jnp.where(first, block(other, i), block(own, i)) for i in range(5)]
    lower = {
        (0, 0): p0[0], (1, 0): p0[1], (1, 1): p0[2],
        (2, 2): p1[0], (3, 2): p1[1], (3, 3): p1[2],
        (2, 0): p0[3], (3, 0): p0[4], (2, 1): p1[3].T, (3, 1): p1[4].T,
    }
    for (i, j), value in lower.items():
        a[at(i, j)] = value
    low[...] = jnp.zeros_like(low)
    inv[...] = jnp.zeros_like(inv)
    factor_step(0, low, inv, a, d, up, ())


def next_kernel(i, low_in, inv_in, a_in, low, inv, a, d, up, mid):
    low[...] = low_in[...]
    inv[...] = inv_in[...]
    a[...] = a_in[...]
    if i == 1:
        tasks = [below_task(a, low, inv, m, 0) for m in (2, 3)]
        tasks += [trail_task(a, low, m, n, 0) for m, n in ((2, 1), (2, 2), (3, 1), (3, 2), (3, 3))]
        tasks += [gather_task(low, inv, mid, 1)]
    else:
        tasks = [below_task(a, low, inv, 3, 1), trail_task(a, low, 3, 2, 1), trail_task(a, low, 3, 3, 1), gather_task(low, inv, mid, 2)]
    factor_step(i, low, inv, a, d, up, tasks)
    invert_task(inv, mid, i)()


def finish_kernel(place, own, other, low_in, inv_in, a_in, low, solved, left, inv, p, d, up, mid):
    first = place[3] == 0
    low[...] = low_in[...]
    inv[...] = inv_in[...]
    p[:, :NB] = jnp.where(first, own[...], other[...])
    p[:, NB:] = jnp.where(first, other[...], own[...])
    left[...] = jnp.zeros_like(left)
    cols = lambda j: (slice(None), pl.ds(j * B, B))

    def solve(j):
        def task():
            solved[cols(j)] = outer(p[cols(j)], inv[at(j, j)])

        return task

    def panel(i, j):
        def task():
            p[cols(i)] = p[cols(i)] - outer(solved[cols(j)], low[at(i, j)])

        return task

    def add(j):
        def task():
            left[:, upto(j + 1)] = left[:, upto(j + 1)] + inner(solved[cols(j)], inv[pl.ds(j * B, B), upto(j + 1)])

        return task

    tasks = [
        solve(0), panel(1, 0), panel(2, 0), panel(3, 0), solve(1), gather_task(low, inv, mid, 3), panel(2, 1), panel(3, 1),
        add(0), solve(2), add(1), panel(3, 2), add(2),
    ]
    d[:B, :] = a_in[at(3, 3)]
    factor_block(d, up, inv.at[at(3, 3)], tasks)
    low[at(3, 3)] = up[...].T
    solve(3)()
    invert_task(inv, mid, 3)()
    add(3)()


def split(value):
    high = value.astype(jnp.bfloat16)
    return high, (value - high.astype(F32)).astype(jnp.bfloat16)


def update_kernel(place, a, left, solved, low, here, beside, across, opposite, out, high, rest):
    row, col, x = place[0], place[1], place[2]
    half = here.shape[1]

    @pl.when(pl.program_id(0) == 0)
    def _():
        for flip, values in ((0, here), (1, beside), (3, across), (2, opposite)):
            q = x ^ flip
            down = jnp.where((q == 1) | (q == 2), NB, 0)
            over = jnp.where(q >= 2, half, 0)
            spot = pl.ds(pl.multiple_of(down, NB), NB), pl.ds(pl.multiple_of(over, half), half)
            high[spot], rest[spot] = split(values[...])

    lh, ll = split(left[...])
    one = lambda u, v: lax.dot_general(u, v, (((1,), (0,)), ((), ())), preferred_element_type=F32)
    product = one(lh, high[...]) + (one(lh, rest[...]) + one(ll, high[...]))
    out[...] = a[...] - product

    @pl.when(col < 2)
    def _():
        out[:, :NB] = solved[:, pl.ds(pl.multiple_of(col * NB, NB), NB)]

    mine = out.shape[0]
    start = pl.program_id(0) * mine

    @pl.when((row < 2) & (start < NB))
    def _():
        out[...] = jnp.zeros_like(out)

    @pl.when((row < 2) & (col < 2) & (start < NB))
    def _():
        out[:, :NB] = low[pl.ds(pl.multiple_of(row * NB + start, B), mine), pl.ds(pl.multiple_of(col * NB, NB), NB)]


SMEM = pl.BlockSpec(memory_space=pltpu.SMEM)
VMEM = pl.BlockSpec(memory_space=pltpu.VMEM)


def call(kernel, outs, scratch, flops, *args):
    shape = lambda s: jax.ShapeDtypeStruct(s, F32)
    return pl.pallas_call(
        kernel,
        out_shape=tuple(shape(s) for s in outs),
        in_specs=[VMEM if v.ndim > 1 else SMEM for v in args],
        out_specs=(VMEM,) * len(outs),
        scratch_shapes=[pltpu.VMEM(s, F32) for s in scratch],
        compiler_params=pltpu.CompilerParams(vmem_limit_bytes=16 << 20),
        cost_estimate=pl.CostEstimate(flops=flops, bytes_accessed=1 << 20, transcendentals=0),
    )(*args)


def update(place, a, left, solved, low, rows):
    n, m = a.shape
    mine = 128
    block = lambda width: pl.BlockSpec((mine, width), lambda i: (i, 0))
    whole = lambda value: pl.BlockSpec(value.shape, lambda i: (0,) * value.ndim)
    return pl.pallas_call(
        update_kernel,
        grid=(n // mine,),
        out_shape=jax.ShapeDtypeStruct(a.shape, F32),
        in_specs=[SMEM, block(m), block(PANEL), block(PANEL), whole(low)] + [whole(v) for v in rows],
        out_specs=block(m),
        scratch_shapes=[pltpu.VMEM((PANEL, m), jnp.bfloat16)] * 2,
        compiler_params=pltpu.CompilerParams(vmem_limit_bytes=16 << 20),
        cost_estimate=pl.CostEstimate(flops=6 * n * m * PANEL, bytes_accessed=12 * n * m, transcendentals=0),
    )(place, a, left, solved, low, *rows)


def on_device(matrix):
    row, col = lax.axis_index("row"), lax.axis_index("col")
    x_index, core = row % NX, col % NK
    place = jnp.stack([row, col, x_index, core]).astype(jnp.int32)
    n = matrix.shape[0]
    half = matrix.shape[1] // 2
    full, block, tall, across, side = (PANEL, PANEL), (B, B), (2 * B, B), (B, PANEL), (n, PANEL)
    cost = 1_500_000_000

    sent = send(matrix[:NB, half:], along_x({0: 3, 1: 2}, lambda z, y, k: z == 0))
    quarter = lambda sent: jnp.where(row < NX, jnp.where(x_index < 2, matrix[:NB, :half], sent), 0.0)
    piece, corner, quarter = corner_tree(corner_piece(matrix[:NB, :NB], row, col), quarter, sent, x_index, core)
    left = jnp.where(col < NK, after(matrix[:, :NB], piece), 0.0)
    left = spread(left, [along_y(h) for h in HOPS[0]])

    quarter, left = pin((quarter, left), corner[0])
    corner = pin(corner, quarter, left)
    beside = send(quarter, along_x({i: i ^ 1 for i in range(NX)}))
    aside = send(quarter, along_x({i: i ^ 3 for i in range(NX)}))
    left = spread(left, [along_y(h) for h in HOPS[1]])
    state = call(first_kernel, [full] * 3, [tall, block], cost, place, *corner)
    state = call(functools.partial(next_kernel, 1), [full] * 3, [tall, block, across], cost, *state)
    beside, left = pin((beside, left), state[0])
    state = pin(state, beside, aside, left)
    opposite = send(beside, along_x({i: i ^ 3 for i in range(NX)}))
    other = send(left, other_core)
    state = call(functools.partial(next_kernel, 2), [full] * 3, [tall, block, across], cost, *state)
    low, solved, own = call(
        finish_kernel, [full, side, side], [full, side, tall, block, across], cost, place, left, other, *state
    )
    return update(place, matrix, own, solved, low, (quarter, beside, aside, opposite))


def solution(mesh):
    return jax.shard_map(on_device, mesh=mesh, in_specs=(P("row", "col"),), out_specs=P("row", "col"), check_vma=False)
```

```python
import functools

import jax
import jax.numpy as jnp
import numpy as np
from jax import lax
from jax.experimental import pallas as pl
from jax.experimental.pallas import tpu as pltpu
from jax.sharding import PartitionSpec as P

NB = 256
PANEL = 512
NZ, NX, NY, NK = 8, 4, 8, 2
B = 128
S = 8
F32 = jnp.float32
BOTH = ("row", "col")


def dot(a, b, dims):
    return lax.dot_general(a, b, (dims, ((), ())), precision=lax.Precision.HIGHEST, preferred_element_type=F32)


def device(z, x, y, k):
    return (((z % NZ) * NX + x % NX) * NY + y % NY) * NK + k


DEVICES = [(z, x, y, k) for z in range(NZ) for x in range(NX) for y in range(NY) for k in range(NK)]


def send(value, target):
    pairs = []
    for at in DEVICES:
        to = target(*at)
        if to is not None:
            pairs.append((device(*at), device(*to)))
    return lax.ppermute(value, BOTH, pairs)


HOPS = [({0: 3}, {0: 5}), ({0: 1, 3: 4, 5: 6}, {0: 7, 3: 2})]


def along_y(part, where=lambda z, x, k: True):
    return lambda z, x, y, k: (z, x, part[y], k) if y in part and where(z, x, k) else None


def along_z(part, where=lambda x, y, k: True):
    return lambda z, x, y, k: (part[z], x, y, k) if z in part and where(x, y, k) else None


def along_x(part, where=lambda z, y, k: True):
    return lambda z, x, y, k: (z, part[x], y, k) if x in part and where(z, y, k) else None


def other_core(z, x, y, k):
    return z, x, y, 1 - k


def spread(value, targets, earlier=None):
    got = [send(value, target) for target in targets]
    if earlier is not None:
        got[0] = after(got[0], earlier)
    return functools.reduce(jnp.add, got, value)


def after(value, *earlier):
    return lax.optimization_barrier((value, *earlier))[0]


def corner_piece(block, row, col):
    blocks = [block[:B, :B], block[B:, :B], block[B:, B:]]
    first, second = [jnp.where(col == 0, x, y) for x, y in zip(blocks, blocks[1:])]
    mine = [jnp.where(row == col, t, h) for t, h in zip(blocks, (first, second, second))]
    return jnp.where((row < 2) & (col < 2), jnp.concatenate(mine), 0.0)


def pin(values, *earlier):
    return lax.optimization_barrier((tuple(values), earlier))[0]


def corner_tree(piece, quarter, sent, x_index, core):
    rounds = [
        [along_z(h, lambda x, y, k: x < 2 and y == 0) for h in HOPS[0]],
        [along_z(h, lambda x, y, k: x < 2 and y == 0) for h in HOPS[1]],
        [along_y(h, lambda z, x, k: x < 2) for h in HOPS[0]],
        [along_y(h, lambda z, x, k: x < 2) for h in HOPS[1]],
    ]
    piece = spread(piece, rounds[0])
    piece = spread(piece, rounds[1], sent)
    quarter = quarter(sent)
    piece = spread(piece, rounds[2])
    quarter = spread(quarter, [along_z(h) for h in HOPS[0]])
    piece = spread(piece, rounds[3], quarter)
    quarter = spread(quarter, [along_z(h) for h in HOPS[1]])
    swap, near, far = [send(piece, along_x(part)) for part in ({0: 1, 1: 0}, {0: 3, 1: 2}, {0: 2, 1: 3})]
    pick = lambda *choices: functools.reduce(lambda v, i: jnp.where(x_index == i, choices[i], v), (1, 2, 3), choices[0])
    even, odd = pick(piece, swap, far, near), pick(swap, piece, near, far)
    triangle = jnp.where(core == 0, even, odd)
    rest = jnp.where(core == 0, odd, even)[: 2 * B]
    mine = jnp.concatenate([triangle, rest])
    return piece, (mine, send(mine, other_core)), quarter


def factor_block(d, up, inv, tasks=()):
    lane = lax.broadcasted_iota(jnp.int32, (S, B), 1)
    sub = lax.broadcasted_iota(jnp.int32, (S, B), 0)
    panels = B // S
    tasks = list(tasks)

    def stack(rows):
        out = rows[0]
        for i in range(1, S):
            out = jnp.where(sub == i, rows[i], out)
        return out

    for done, k in enumerate(range(0, B, S)):
        here = (lane >= k) & (lane < k + S)
        p = [jnp.broadcast_to(d[k + i : k + i + 1, :], (S, B)) for i in range(S)]
        spare = B + done % 2 * S * S
        for j in range(S):
            d[spare + j * S : spare + (j + 1) * S, :] = jnp.broadcast_to(d[k : k + S, k + j : k + j + 1], (S, B))
        element = lambda i, j: d[spare + j * S + i : spare + j * S + i + 1, :]
        s = {(i, j): jnp.broadcast_to(element(i, j), (S, B)) for i in range(S) for j in range(i + 1)}
        r, w = [], {}
        for j in range(S):
            r.append(lax.rsqrt(s[j, j]))
            for i in range(j + 1, S):
                s[i, j] = s[i, j] * r[j]
            for i in range(j + 1, S):
                for m in range(j + 1, i + 1):
                    s[i, m] = s[i, m] - s[i, j] * s[m, j]
            w[j, j] = r[j]
            for m in range(j):
                acc = s[j, m] * w[m, m]
                for q in range(m + 1, j):
                    acc = acc + s[j, q] * w[q, m]
                w[j, m] = -r[j] * acc
        q = [jnp.where(here, jnp.where(lane == k + i, 1.0, 0.0), p[i]) for i in range(S)]
        u, t = [], []
        for i in range(S):
            a = w[i, 0] * q[0]
            b = w[i, 0] * p[0]
            for m in range(1, i + 1):
                a = a + w[i, m] * q[m]
                b = b + w[i, m] * p[m]
            u.append(a)
            t.append(b)
        up[k : k + S, :] = jnp.where(lane >= k + sub, stack(t), 0.0)
        inv[k : k + S, :] = jnp.where(lane <= k + sub, stack(u), 0.0)
        rest = B - k - S
        if rest:
            below = d[k + S : B, :]
            groups = rest // S
            new = jnp.where(here[None], 0.0, below.reshape(groups, S, B))
            for i in range(S):
                v = w[i, i] * u[i]
                for m in range(i + 1, S):
                    v = v + w[m, i] * u[m]
                c = jnp.broadcast_to(below[:, k + i : k + i + 1], (rest, B)).reshape(groups, S, B)
                new = new - c * v[None]
            d[k + S : B, :] = new.reshape(rest, B)
        for task in tasks[len(tasks) * done // panels : len(tasks) * (done + 1) // panels]:
            task()


def at(i, j):
    return pl.ds(i * B, B), pl.ds(j * B, B)


def split(value):
    high = value.astype(jnp.bfloat16)
    return high, (value - high.astype(F32)).astype(jnp.bfloat16)


def product(a, b, dims):
    one = lambda u, v: lax.dot_general(u, v, (dims, ((), ())), preferred_element_type=F32)
    (ah, al), (bh, bl) = split(a), split(b)
    return one(ah, bh) + (one(ah, bl) + one(al, bh))


def outer(a, b):
    return dot(a, b, ((1,), (1,)))


def inner(a, b):
    return dot(a, b, ((1,), (0,)))


def below_task(a, low, inv, i, j):
    def task():
        low[at(i, j)] = outer(a[at(i, j)], inv[at(j, j)])

    return task


def trail_task(a, low, i, j, p):
    def task():
        a[at(i, j)] = a[at(i, j)] - outer(low[at(i, p)], low[at(j, p)])

    return task


def upto(i):
    return pl.ds(0, i * B)


def gather_task(low, inv, mid, i):
    def task():
        mid[:, upto(i)] = inner(low[pl.ds(i * B, B), upto(i)], inv[upto(i), upto(i)])

    return task


def invert_task(inv, mid, i):
    def task():
        inv[pl.ds(i * B, B), upto(i)] = -inner(inv[at(i, i)], mid[:, upto(i)])

    return task


def factor_step(i, low, inv, a, d, up, tasks):
    d[:B, :] = a[at(i, i)]
    factor_block(d, up, inv.at[at(i, i)], tasks)
    low[at(i, i)] = up[...].T
    if i < 3:
        below_task(a, low, inv, i + 1, i)()
        trail_task(a, low, i + 1, i + 1, i)()


def first_kernel(place, own, other, low, inv, a, d, up, mid):
    first = place[3] == 0
    block = lambda ref, i: ref[i * B : (i + 1) * B, :]
    p0 = [jnp.where(first, block(own, i), block(other, i)) for i in range(5)]
    p1 = [jnp.where(first, block(other, i), block(own, i)) for i in range(5)]
    lower = {
        (0, 0): p0[0], (1, 0): p0[1], (1, 1): p0[2],
        (2, 2): p1[0], (3, 2): p1[1], (3, 3): p1[2],
        (2, 0): p0[3], (3, 0): p0[4], (2, 1): p1[3].T, (3, 1): p1[4].T,
    }
    for (i, j), value in lower.items():
        a[at(i, j)] = value
    low[...] = jnp.zeros_like(low)
    inv[...] = jnp.zeros_like(inv)
    factor_step(0, low, inv, a, d, up, ())
    tasks = [below_task(a, low, inv, m, 0) for m in (2, 3)]
    tasks += [trail_task(a, low, m, n, 0) for m, n in ((2, 1), (2, 2), (3, 1), (3, 2), (3, 3))]
    factor_step(1, low, inv, a, d, up, tasks + [gather_task(low, inv, mid, 1)])
    invert_task(inv, mid, 1)()


def next_kernel(low_in, inv_in, a_in, low, inv, a, d, up, mid):
    low[...] = low_in[...]
    inv[...] = inv_in[...]
    a[...] = a_in[...]
    tasks = [below_task(a, low, inv, 3, 1), trail_task(a, low, 3, 2, 1), trail_task(a, low, 3, 3, 1), gather_task(low, inv, mid, 2)]
    factor_step(2, low, inv, a, d, up, tasks)
    invert_task(inv, mid, 2)()


def finish_kernel(place, own, other, low_in, inv_in, a_in, low, solved, left, inv, p, d, up, mid):
    first = place[3] == 0
    low[...] = low_in[...]
    inv[...] = inv_in[...]
    p[:, :NB] = jnp.where(first, own[...], other[...])
    p[:, NB:] = jnp.where(first, other[...], own[...])
    cols = lambda j: (slice(None), pl.ds(j * B, B))

    def solve(j):
        def task():
            solved[cols(j)] = product(p[cols(j)], inv[at(j, j)], ((1,), (1,)))

        return task

    def panel(i, j):
        def task():
            p[cols(i)] = p[cols(i)] - product(solved[cols(j)], low[at(i, j)], ((1,), (1,)))

        return task

    def add(j):
        def task():
            term = product(solved[cols(j)], inv[pl.ds(j * B, B), upto(j + 1)], ((1,), (0,)))
            if j:
                left[:, upto(j)] = left[:, upto(j)] + term[:, : j * B]
            left[cols(j)] = term[:, j * B :]

        return task

    tasks = [
        solve(0), panel(1, 0), panel(2, 0), panel(3, 0), solve(1), gather_task(low, inv, mid, 3), panel(2, 1), panel(3, 1),
        add(0), solve(2), add(1), panel(3, 2), add(2),
    ]
    d[:B, :] = a_in[at(3, 3)]
    factor_block(d, up, inv.at[at(3, 3)], tasks)
    low[at(3, 3)] = up[...].T
    solve(3)()
    invert_task(inv, mid, 3)()
    add(3)()


def update_kernel(place, a, left, solved, low, here, beside, across, opposite, out, high, rest):
    row, col, x = place[0], place[1], place[2]
    half = here.shape[1]

    @pl.when(pl.program_id(0) == 0)
    def _():
        for flip, values in ((0, here), (1, beside), (3, across), (2, opposite)):
            q = x ^ flip
            down = jnp.where((q == 1) | (q == 2), NB, 0)
            over = jnp.where(q >= 2, half, 0)
            spot = pl.ds(pl.multiple_of(down, NB), NB), pl.ds(pl.multiple_of(over, half), half)
            high[spot], rest[spot] = split(values[...])

    lh, ll = split(left[...])
    one = lambda u, v: lax.dot_general(u, v, (((1,), (0,)), ((), ())), preferred_element_type=F32)
    product = one(lh, high[...]) + (one(lh, rest[...]) + one(ll, high[...]))
    out[...] = a[...] - product

    @pl.when(col < 2)
    def _():
        out[:, :NB] = solved[:, pl.ds(pl.multiple_of(col * NB, NB), NB)]

    mine = out.shape[0]
    start = pl.program_id(0) * mine

    @pl.when((row < 2) & (start < NB))
    def _():
        out[...] = jnp.zeros_like(out)

    @pl.when((row < 2) & (col < 2) & (start < NB))
    def _():
        out[:, :NB] = low[pl.ds(pl.multiple_of(row * NB + start, B), mine), pl.ds(pl.multiple_of(col * NB, NB), NB)]


SMEM = pl.BlockSpec(memory_space=pltpu.SMEM)
VMEM = pl.BlockSpec(memory_space=pltpu.VMEM)


def call(kernel, outs, scratch, flops, *args):
    shape = lambda s: jax.ShapeDtypeStruct(s, F32)
    return pl.pallas_call(
        kernel,
        out_shape=tuple(shape(s) for s in outs),
        in_specs=[VMEM if v.ndim > 1 else SMEM for v in args],
        out_specs=(VMEM,) * len(outs),
        scratch_shapes=[pltpu.VMEM(s, F32) for s in scratch],
        compiler_params=pltpu.CompilerParams(vmem_limit_bytes=16 << 20),
        cost_estimate=pl.CostEstimate(flops=flops, bytes_accessed=1 << 20, transcendentals=0),
    )(*args)


def update(place, a, left, solved, low, rows):
    n, m = a.shape
    mine = 256
    block = lambda width: pl.BlockSpec((mine, width), lambda i: (i, 0))
    whole = lambda value: pl.BlockSpec(value.shape, lambda i: (0,) * value.ndim)
    return pl.pallas_call(
        update_kernel,
        grid=(n // mine,),
        out_shape=jax.ShapeDtypeStruct(a.shape, F32),
        in_specs=[SMEM, block(m), block(PANEL), block(PANEL), whole(low)] + [whole(v) for v in rows],
        out_specs=block(m),
        scratch_shapes=[pltpu.VMEM((PANEL, m), jnp.bfloat16)] * 2,
        compiler_params=pltpu.CompilerParams(vmem_limit_bytes=16 << 20),
        cost_estimate=pl.CostEstimate(flops=6 * n * m * PANEL, bytes_accessed=12 * n * m, transcendentals=0),
    )(place, a, left, solved, low, *rows)


def on_device(matrix):
    row, col = lax.axis_index("row"), lax.axis_index("col")
    x_index, core = row % NX, col % NK
    place = jnp.stack([row, col, x_index, core]).astype(jnp.int32)
    n = matrix.shape[0]
    half = matrix.shape[1] // 2
    full, block, tall, across, side = (PANEL, PANEL), (B, B), (2 * B, B), (B, PANEL), (n, PANEL)
    cost = 1_500_000_000

    sent = send(matrix[:NB, half:], along_x({0: 3, 1: 2}, lambda z, y, k: z == 0))
    quarter = lambda sent: jnp.where(row < NX, jnp.where(x_index < 2, matrix[:NB, :half], sent), 0.0)
    piece, corner, quarter = corner_tree(corner_piece(matrix[:NB, :NB], row, col), quarter, sent, x_index, core)
    left = jnp.where(col < NK, after(matrix[:, :NB], piece), 0.0)
    left = spread(left, [along_y(h) for h in HOPS[0]])

    quarter, left = pin((quarter, left), corner[0])
    corner = pin(corner, quarter, left)
    beside = send(quarter, along_x({i: i ^ 1 for i in range(NX)}))
    aside = send(quarter, along_x({i: i ^ 3 for i in range(NX)}))
    left = spread(left, [along_y(h) for h in HOPS[1]])
    state = call(first_kernel, [full] * 3, [tall, block, across], 2 * cost, place, *corner)
    beside, left = pin((beside, left), state[0])
    state = pin(state, beside, aside, left)
    opposite = send(beside, along_x({i: i ^ 3 for i in range(NX)}))
    other = send(left, other_core)
    state = call(next_kernel, [full] * 3, [tall, block, across], cost, *state)
    low, solved, own = call(
        finish_kernel, [full, side, side], [full, side, tall, block, across], cost, place, left, other, *state
    )
    return update(place, matrix, own, solved, low, (quarter, beside, aside, opposite))


def solution(mesh):
    return jax.shard_map(on_device, mesh=mesh, in_specs=(P("row", "col"),), out_specs=P("row", "col"), check_vma=False)
```
